256 devices in a mesh: exp: 64 (over z, y, core), voc: 4 (over x).
Axes of the slice: x: 4, y: 4, z: 8, core: 2. Of those that a mesh axis runs over, the one named last changes fastest.
Arguments:
- tokens: bfloat16 [2048, 4096], P('exp', 'voc'), may hold values from -6 to 6
- expert_routes: int32 [2048, 2], P('exp'), may hold values from 0 to 7, all different within a row; in each aligned block of 32 rows (0 to 31, 32 to 63, ...) at most 16 rows name the same one
- gate_scores: float32 [2048, 2], P('exp'), may hold values from 0.2 to 1
- w_gate: bfloat16 [64, 4096, 1792], P('exp', None, 'voc'), may hold values from -0.09375 to 0.09375
- w_up: bfloat16 [64, 4096, 1792], P('exp', None, 'voc'), may hold values from -0.09375 to 0.09375
- w_down: bfloat16 [64, 1792, 4096], P('exp', 'voc'), may hold values from -0.046875 to 0.046875
- head_weight: bfloat16 [4096, 32000], P('voc', 'exp'), may hold values from -0.09375 to 0.09375
- passage_ids: int32 [64, 32], replicated, may hold values from 0 to 3, never falling along the last dimension, each value on 1 to 16 neighbouring positions
- doc_length: int32 [64, 4], replicated, may hold values from 20 to 180, as said below
Outputs:
- term_scores: float32 [256, 32000], P('voc', 'exp')
The draws below stay inside these ranges and needn't reach their ends.
Inputs may be any that keep to these rules, and one draw needn't show every extreme that they name: `expert_routes`: each row names 2 different experts; among the rows of one exp index (32 tokens) no expert is named more than 16 times. `passage_ids`: never falling along a row; every passage holds 1 to 16 tokens. `doc_length`: positive whole numbers of words.
All inputs are finite; a program needn't handle non-finite values.
Results may differ from the reference program's by a relative error of at most 0.0065.
Values may be sent and summed in bfloat16 or wider, within the bound.
A program may use at most 128 MiB of HBM per device.

```python
import math
import jax
import jax.numpy as jnp
import numpy as np
from jax import lax

D = 4096
FF = 14336
EXPERTS = 8
VOCAB = 32000
TOP_K = 2
TOK_DEV = 32
PASS_DEV = 4
CAP = 16
GROUP = 8
SHARDS = 64
TOKENS = 2048
PASSAGES = 256
N_EXP = 64
N_VOC = 4


def draw_doc_length(key, part):
    key = jax.random.fold_in(key, 7)
    base = jax.random.randint(key, (SHARDS, PASS_DEV), 20, 61)
    shard_index = lax.broadcasted_iota(jnp.int32, (SHARDS, PASS_DEV), 0)
    pass_index = lax.broadcasted_iota(jnp.int32, (SHARDS, PASS_DEV), 1)
    top_cell = (shard_index == SHARDS - 1) & (pass_index == 0)
    low_cell = (shard_index == 0) & (pass_index == PASS_DEV - 1)
    base = jnp.where(top_cell, 60, base)
    base = jnp.where(low_cell, 20, base)
    return (base * (SHARDS - 1 + 2 * shard_index) // (SHARDS - 1)).astype(jnp.int32)


def steps_of(own_key, extent, cuts, smallest, high):
    loudness, own = 1.0, jax.random.fold_in(own_key, 6)
    for dim, blocks in cuts:
        steps = jnp.exp(jax.random.uniform(jax.random.fold_in(own, dim), (blocks,), jnp.float32, smallest / len(cuts), high / len(cuts)))
        loudness = loudness * jnp.repeat(steps, extent[dim] // blocks).reshape([-1 if axis == dim else 1 for axis in range(len(extent))])
    return loudness


def length_profile(count, total, limit, lean):
    portions = [(1 << 20) // math.isqrt(grade ** lean) + 1 for grade in range(2, count + 1)]
    surplus, given = total - limit - (count - 1), [1] * (count - 1)
    while surplus > 0:
        candidates = [i for i in range(count - 1) if given[i] < limit]
        pool, left = sum([portions[i] for i in candidates]), surplus
        for i in candidates:
            more = min(limit - given[i], max(1, left * portions[i] // pool), surplus)
            given[i] = given[i] + more
            surplus = surplus - more
    return np.array([limit] + given)


def uneven(rng, amount, total, limit, lean):
    if amount == 2:
        one = jax.random.randint(rng, (), max(1, total - limit), min(limit, total - 1) + 1)
        return jnp.stack([one, total - one])
    tallies = jnp.asarray(length_profile(amount, total, limit, lean), jnp.int32)
    pairs = (amount - 1) // 2
    source_of, receiver = tallies[1:1 + 2 * pairs:2], tallies[2:2 + 2 * pairs:2]
    margin = jnp.minimum(source_of - 1, limit - receiver)
    passed = jax.random.randint(jax.random.fold_in(rng, 1), (pairs,), 0, 1 << 20) % (margin + 1)
    tallies = tallies.at[1:1 + 2 * pairs:2].set(source_of - passed).at[2:2 + 2 * pairs:2].set(receiver + passed)
    return tallies[jax.random.permutation(jax.random.fold_in(rng, 2), amount)]


def assign_block(own_key, own, number, rows, count, top, limit, slope):
    ranking = jax.random.permutation(own_key, count)
    packed, common = load_shares(count, rows * top, limit, slope, True), load_shares(count, rows * top, limit, slope, False)
    places = jnp.arange(count)

    def named(sizes, rotation):
        used = int((sizes > 0).sum())
        fixed = max(1, used // 4)
        passed = fixed + (places - fixed + rotation * (used - fixed)) % max(1, count - fixed)
        return jnp.zeros((count,), jnp.int32).at[ranking[jnp.where(places < fixed, places, passed)]].set(jnp.asarray(sizes, jnp.int32))

    sizes = jnp.where(number % 4 == 0, named(packed, number // 4), named(common, number - number // 4 - 1))
    mixed = jax.random.permutation(jax.random.fold_in(own, 3), count)
    source_of, taker = mixed[0:count // 2 * 2:2], mixed[1:count // 2 * 2:2]
    slack = jnp.minimum(sizes[source_of] - 1, limit - sizes[taker]) // 2
    slack = jnp.where((source_of == ranking[0]) | (taker == ranking[0]) | (sizes[taker] == 0), 0, jnp.maximum(slack, 0))
    passed = jax.random.randint(jax.random.fold_in(own, 4), (count // 2,), 0, 1 << 20) % (slack + 1)
    sizes = sizes.at[source_of].add(-passed).at[taker].add(passed)
    items = jnp.searchsorted(jnp.cumsum(sizes), jnp.arange(rows * top), side="right").astype(jnp.int32)
    table = items.reshape(top, rows).T
    table = table[jax.random.permutation(jax.random.fold_in(own, 1), rows)]
    rotation = jax.random.randint(jax.random.fold_in(own, 2), (rows, 1), 0, top)
    return jnp.take_along_axis(table, (jnp.arange(top)[None, :] + rotation) % top, axis=1)


def load_shares(amount, total, bound, lean, full):
    weights = [(1 << 20) // math.isqrt(rank ** lean) + 1 for rank in range(1, amount + 1)]
    largest = bound if full else min(bound, max(-(-total // amount), total * weights[0] // sum(weights)))
    least = 1 if total - largest >= amount - 1 else 0
    counts, spare = [largest] + [least] * (amount - 1), total - largest - least * (amount - 1)
    while spare > 0:
        free = [i for i in range(1, amount) if counts[i] < largest] or [i for i in range(1, amount) if counts[i] < bound]
        mass, remaining = sum([weights[i] for i in free]), spare
        for i in free:
            addition = min(bound - counts[i], max(1, remaining * weights[i] // mass), spare)
            counts[i] = counts[i] + addition
            spare = spare - addition
    return np.array(counts)


def scatter_about(rng, extent, spread, bound, cuts=(), kind=jnp.bfloat16):
    values = spread * jax.random.normal(rng, extent, jnp.float32)
    if cuts:
        values = values * steps_of(rng, extent, cuts, -0.22, 0.18)
    return jnp.clip(values, -bound, bound).astype(kind)


def setup_inputs(seed: int = 0) -> dict:
    seeds = jax.random.split(jax.random.key(seed), 10)
    tokens = scatter_about(seeds[0], (TOKENS, D), 1.0, 6.0, ((0, 64), (1, 4)))
    expert_routes_keys = jax.random.split(jax.random.fold_in(seeds[1], 1), TOKENS // TOK_DEV)
    expert_routes_turns = jax.random.permutation(jax.random.fold_in(seeds[1], 3), TOKENS // TOK_DEV)
    expert_routes = jax.vmap(lambda own, number: assign_block(jax.random.fold_in(seeds[1], 2), own, number, TOK_DEV, EXPERTS, TOP_K, CAP, 2))(expert_routes_keys, expert_routes_turns).reshape((TOKENS, TOP_K))
    gate_scores = jnp.clip(0.2 + 0.8 * jax.random.uniform(seeds[2], (TOKENS, TOP_K), jnp.float32) ** steps_of(seeds[2], (TOKENS, TOP_K), ((0, 64),), -0.2, 0.2), 0.2, 1.0)
    w_gate = scatter_about(seeds[3], (N_EXP, D, FF // GROUP), D ** -0.5, 0.09375, ((0, 64), (2, 4)))
    w_up = scatter_about(seeds[4], (N_EXP, D, FF // GROUP), D ** -0.5, 0.09375, ((0, 64), (2, 4)))
    w_down = scatter_about(seeds[5], (N_EXP, FF // GROUP, D), FF ** -0.5, 0.046875, ((0, 64), (1, 4)))
    head_weight = scatter_about(seeds[6], (D, VOCAB), D ** -0.5, 0.09375, ((0, 4), (1, 64)))
    passage_ids = jax.vmap(lambda own: jnp.searchsorted(jnp.cumsum(uneven(own, PASS_DEV, TOK_DEV, CAP, 2)), jnp.arange(TOK_DEV), side="right"))(jax.random.split(seeds[7], SHARDS)).reshape((SHARDS, TOK_DEV)).astype(jnp.int32)
    doc_length = draw_doc_length(jax.random.fold_in(seeds[9], 71), 0)
    return dict(tokens=tokens, expert_routes=expert_routes, gate_scores=gate_scores, w_gate=w_gate, w_up=w_up, w_down=w_down, head_weight=head_weight, passage_ids=passage_ids, doc_length=doc_length)


def slot_tables(route_rows, gate_rows):
    count = route_rows.shape[0]
    expert_ids = jnp.arange(EXPERTS, dtype=jnp.int32)
    hit_table = (route_rows[:, :, None] == expert_ids).astype(jnp.int32)
    flat_hits = hit_table.reshape(count * TOP_K, EXPERTS)
    rank_table = jnp.cumsum(flat_hits, axis=0) - flat_hits
    slot_table = jnp.sum(flat_hits * rank_table, axis=1).reshape(count, TOP_K)
    slot_ids = jnp.arange(CAP, dtype=jnp.int32)
    matches = hit_table[:, :, :, None] * (slot_table[:, :, None, None] == slot_ids).astype(jnp.int32)
    place_table = jnp.sum(matches, axis=1)
    gate_table = jnp.sum(matches.astype(jnp.float32) * gate_rows[:, :, None, None], axis=1)
    return place_table, gate_table


def reference(tokens, expert_routes, gate_scores, w_gate, w_up, w_down, head_weight, passage_ids, doc_length):
    tok_shards = tokens.reshape(SHARDS, TOK_DEV, D)
    route_shards = expert_routes.reshape(SHARDS, TOK_DEV, TOP_K)
    gate_shards = gate_scores.reshape(SHARDS, TOK_DEV, TOP_K)
    place_table, gate_table = jax.vmap(slot_tables)(route_shards, gate_shards)
    width_part = FF // (GROUP * N_VOC)

    def expert_out(expert):
        picks = lax.dynamic_index_in_dim(place_table, expert, 2, keepdims=False).astype(jnp.float32)
        slot_rows = jnp.einsum("stc,std->scd", picks, tok_shards.astype(jnp.float32)).astype(jnp.bfloat16)
        slot_rows = slot_rows.reshape(SHARDS * CAP, D)

        def member_out(member):
            row_index = expert * GROUP + member
            gate_local = lax.dynamic_index_in_dim(w_gate, row_index, 0, keepdims=False)
            up_local = lax.dynamic_index_in_dim(w_up, row_index, 0, keepdims=False)
            down_local = lax.dynamic_index_in_dim(w_down, row_index, 0, keepdims=False)
            total = jnp.zeros((SHARDS * CAP, D), jnp.float32)
            for quarter in range(N_VOC):
                low = quarter * width_part
                gate_pre = jnp.dot(slot_rows, gate_local[:, low:low + width_part], preferred_element_type=jnp.float32)
                up_pre = jnp.dot(slot_rows, up_local[:, low:low + width_part], preferred_element_type=jnp.float32)
                hidden = (jax.nn.silu(gate_pre) * up_pre).astype(jnp.bfloat16)
                part = jnp.dot(hidden, down_local[low:low + width_part, :], preferred_element_type=jnp.float32)
                total = total + lax.optimization_barrier(part.astype(jnp.bfloat16)).astype(jnp.float32)
            return total.astype(jnp.bfloat16)

        members = lax.map(member_out, jnp.arange(GROUP, dtype=jnp.int32))
        return jnp.sum(members.astype(jnp.float32), axis=0).reshape(SHARDS, CAP, D)

    member_sum = lax.map(expert_out, jnp.arange(EXPERTS, dtype=jnp.int32))
    moe = jnp.einsum("stec,escd->std", gate_table, member_sum, precision=lax.Precision.HIGHEST)
    layer_out = (tok_shards.astype(jnp.float32) + moe).astype(jnp.bfloat16)
    avg_length = jnp.sum(doc_length.astype(jnp.float32)) / PASSAGES

    def shard_scores(items):
        rows_here, ids_here, lengths_here = items
        logits = jnp.dot(rows_here, head_weight, preferred_element_type=jnp.float32)
        saturated = jnp.log1p(jnp.maximum(logits, 0.0))
        one_hot = (ids_here[None, :] == jnp.arange(PASS_DEV, dtype=jnp.int32)[:, None]).astype(jnp.float32)
        freq = jnp.dot(one_hot, saturated, precision=lax.Precision.HIGHEST)
        scale = 1.0 - 0.75 + 0.75 * lengths_here.astype(jnp.float32) / avg_length
        return freq * (1.2 + 1.0) / (freq + 1.2 * scale[:, None])

    scores = lax.map(shard_scores, (layer_out, passage_ids, doc_length))
    return scores.reshape(PASSAGES, VOCAB)
```

```python
import jax
import jax.numpy as jnp
from jax import lax
from jax.experimental import pallas as pl
from jax.experimental.pallas import tpu as pltpu
from jax.sharding import PartitionSpec as P

MESH = pl.DeviceIdType.MESH
BF16, F32 = jnp.bfloat16, jnp.float32
EXPERTS = 8
CAP = 16
TOK = 32
WIDTH = 1024
FEATURES = 4096
CHUNKS = 4
PASSAGES_HERE = 64
SENDS = 320
NT = (((1,), (1,)), ((), ()))


def aligned(value, step):
    return pl.multiple_of(value, step)


def kernel(
    tok, routes, gates, w_gate, w_up, w_down, head, ids, lengths, out,
    X, PART, PREC, S, RA, RB, TA, TB, RA2, RB2, U, RET, SLOT, WG, WU, WD, HW, LG, LS, LR,
    send_sem, recv_sem, local_sem,
):
    index = lax.axis_index("exp")
    x = lax.axis_index("voc")
    z, y, c = index // 8, (index // 2) % 4, index % 2

    def at(dx=0, dy=0, dz=0, dc=0):
        return (((z + dz) % 8) * 8 + ((y + dy) % 4) * 2 + (c + dc) % 2, (x + dx) % 4)

    weights = [
        pltpu.make_async_copy(src, dst, local_sem.at[i])
        for i, (src, dst) in enumerate([(w_gate, WG), (w_up, WU), (w_down, WD), (head, HW)])
    ]
    for copy in weights:
        copy.start()

    partners = (
        [at(dx=i) for i in (1, 2, 3)]
        + [at(dy=i) for i in (1, 2, 3)]
        + [at(dz=i) for i in range(1, 8)]
        + [at(dc=1)]
    )
    barrier = pltpu.get_barrier_semaphore()
    for partner in partners:
        pl.semaphore_signal(barrier, inc=1, device_id=partner, device_id_type=MESH)

    slot_row = lax.broadcasted_iota(jnp.int32, (EXPERTS * CAP, TOK), 0)
    expert_of, slot_of = slot_row // CAP, slot_row % CAP
    first, second = routes[0:1, :] == expert_of, routes[1:2, :] == expert_of
    hit = (first | second).astype(F32)
    earlier = (
        lax.broadcasted_iota(jnp.int32, (TOK, TOK), 0)
        < lax.broadcasted_iota(jnp.int32, (TOK, TOK), 1)
    ).astype(F32)
    rank = jnp.dot(hit.astype(BF16), earlier.astype(BF16), preferred_element_type=F32)
    place = jnp.where(rank == slot_of.astype(F32), hit, 0.0)
    SLOT[...] = jnp.dot(place.astype(BF16), tok[...], preferred_element_type=F32).astype(BF16)
    gate_of = place * (jnp.where(first, gates[0:1, :], 0.0) + jnp.where(second, gates[1:2, :], 0.0))

    pl.semaphore_wait(barrier, len(partners))

    copies = []

    def send(src, dst, target):
        n = len(copies)
        copy = pltpu.make_async_remote_copy(
            src_ref=src, dst_ref=dst, send_sem=send_sem.at[n], recv_sem=recv_sem.at[n],
            device_id=target, device_id_type=MESH,
        )
        copy.start()
        copies.append(copy)
        return copy

    def arrived(group):
        for copy in group:
            copy.wait_recv()

    my_cols = pl.ds(aligned(x * WIDTH, WIDTH), WIDTH)

    def cols(i):
        return pl.ds(aligned(((x + i) % 4) * WIDTH, WIDTH), WIDTH)

    def rows(k, u, core, yy, count):
        return pl.ds(aligned(((k * 2 + u) * 2 + core) * 64 + yy * CAP, CAP), count)

    def block(k, u):
        return X.at[rows(k, u, c, y, CAP), my_cols]

    from_z = {}
    for k in range(CHUNKS):
        for u, d in ((0, k), (1, 7 - k)):
            if d == 0:
                X[rows(k, u, c, y, CAP), my_cols] = SLOT[pl.ds(aligned(z * CAP, CAP), CAP), :]
                from_z[k, u] = []
            else:
                src = SLOT.at[pl.ds(aligned(((z + d) % 8) * CAP, CAP), CAP), :]
                from_z[k, u] = [send(src, block(k, u), at(dz=d))]

    a1, a2, a3, d1, r1, r2, r3 = {}, {}, {}, {}, {}, {}, {}

    def gather_first(k):
        arrived(from_z[k, 0])
        a1[k] = [send(block(k, 0), block(k, 0), at(dx=i)) for i in (2, 1, 3)]
        arrived(from_z[k, 1])
        a1[k] += [send(block(k, 1), block(k, 1), at(dy=i)) for i in (2, 1, 3)]

    def gather_second(k):
        arrived(a1[k])
        ours = X.at[rows(k, 0, c, y, CAP), :]
        a2[k] = [send(ours, ours, at(dy=i)) for i in (2, 1, 3)]
        ours = X.at[rows(k, 1, c, 0, 64), my_cols]
        a2[k] += [send(ours, ours, at(dx=i)) for i in (2, 1, 3)]

    def gather_cores(k):
        arrived(a2[k])
        a3[k] = []
        for u in (0, 1):
            ours = X.at[rows(k, u, c, 0, 64), :]
            a3[k].append(send(ours, ours, at(dc=1)))

    hidden = {}

    def gate_up(k):
        arrived(a3[k])
        here = X[k * 256 : (k + 1) * 256, :]
        gate_pre = lax.dot_general(here, WG[...], NT, preferred_element_type=F32)
        up_pre = lax.dot_general(here, WU[...], NT, preferred_element_type=F32)
        hidden[k] = (gate_pre / (1.0 + jnp.exp(-gate_pre)) * up_pre).astype(BF16)

    def down(k):
        for n in range(4):
            part = slice(n * WIDTH, (n + 1) * WIDTH)
            PART[k * 256 : (k + 1) * 256, part] = jnp.dot(
                hidden[k], WD[:, part], preferred_element_type=F32
            ).astype(BF16)
        d1[k] = [
            send(PART.at[rows(k, u, 1 - c, 0, 64), :], PREC.at[pl.ds((k * 2 + u) * 64, 64), :], at(dc=1))
            for u in (0, 1)
        ]

    def reduce_first(k):
        arrived(d1[k])
        for u in (0, 1):
            to = pl.ds((k * 2 + u) * 64, 64)
            S[to, :] = (
                PART[rows(k, u, c, 0, 64), :].astype(F32) + PREC[to, :].astype(F32)
            ).astype(BF16)
        r1[k] = []
        for i in (2, 1, 3):
            src = S.at[pl.ds(aligned(k * 128 + ((y + i) % 4) * CAP, CAP), CAP), :]
            r1[k].append(send(src, RA.at[k, i - 1], at(dy=i)))
            src = S.at[pl.ds(k * 128 + 64, 64), cols(i)]
            r1[k].append(send(src, RB.at[k, i - 1], at(dx=i)))

    def reduce_second(k):
        arrived(r1[k])
        total = S[pl.ds(aligned(k * 128 + y * CAP, CAP), CAP), :].astype(F32)
        for i in range(3):
            total = total + RA[k, i].astype(F32)
        TA[k] = total.astype(BF16)
        total = S[k * 128 + 64 : k * 128 + 128, my_cols].astype(F32)
        for i in range(3):
            total = total + RB[k, i].astype(F32)
        TB[k] = total.astype(BF16)
        r2[k] = []
        for i in (2, 1, 3):
            r2[k].append(send(TA.at[k, :, cols(i)], RA2.at[k, i - 1], at(dx=i)))
            src = TB.at[k, pl.ds(aligned(((y + i) % 4) * CAP, CAP), CAP), :]
            r2[k].append(send(src, RB2.at[k, i - 1], at(dy=i)))

    mine = pl.ds(aligned(z * CAP, CAP), CAP)

    def give_back(k):
        arrived(r2[k])
        r3[k] = []
        for u, (own, more) in enumerate(
            [
                (TA[k, :, my_cols], RA2),
                (TB[k, pl.ds(aligned(y * CAP, CAP), CAP), :], RB2),
            ]
        ):
            total = own.astype(F32)
            for i in range(3):
                total = total + more[k, i].astype(F32)
            if u == 0 and k == 0:
                RET[mine, :] = total.astype(BF16)
            else:
                U[k, u] = total.astype(BF16)
                dz = -k if u == 0 else 1 + k
                r3[k].append(send(U.at[k, u], RET.at[mine, :], at(dz=dz % 8)))

    gather_first(0)
    gather_first(1)
    gather_second(0)
    gather_first(2)
    gather_second(1)
    gather_first(3)
    gather_cores(0)
    gather_second(2)
    for copy in weights[:3]:
        copy.wait()
    gate_up(0)
    gather_cores(1)
    gather_second(3)
    down(0)
    gate_up(1)
    reduce_first(0)
    gather_cores(2)
    down(1)
    gate_up(2)
    reduce_first(1)
    gather_cores(3)
    reduce_second(0)
    down(2)
    gate_up(3)
    reduce_first(2)
    give_back(0)
    reduce_second(1)
    down(3)
    give_back(1)
    reduce_second(2)
    reduce_first(3)
    give_back(2)
    reduce_second(3)
    give_back(3)

    eye = (
        lax.broadcasted_iota(jnp.int32, (TOK, TOK), 0)
        == lax.broadcasted_iota(jnp.int32, (TOK, TOK), 1)
    ).astype(F32)
    highest = lax.Precision.HIGHEST
    gate_table = lax.dot_general(eye, gate_of, NT, precision=highest, preferred_element_type=F32)
    for k in range(CHUNKS):
        arrived(r3[k])
    moe = jnp.dot(gate_table, RET[...].astype(F32), precision=highest, preferred_element_type=F32)
    LG[z, y, c] = (tok[...].astype(F32) + moe).astype(BF16)

    ours = LG.at[z, y, c]
    to_planes = [send(ours, ours, at(dz=d)) for d in (4, 3, 5, 2, 6, 1, 7)]

    passage = lax.broadcasted_iota(jnp.int32, (PASSAGES_HERE, 64), 0)
    pick = (lax.broadcasted_iota(jnp.int32, (PASSAGES_HERE, 64), 1) == passage // 4 + 16 * x).astype(F32)
    ids_of = lax.dot_general(pick, ids[...].astype(F32), NT, precision=highest, preferred_element_type=F32)
    spread = (
        lax.broadcasted_iota(jnp.int32, (TOK, 512), 1) % TOK
        == lax.broadcasted_iota(jnp.int32, (TOK, 512), 0)
    ).astype(F32)
    ids_of = jnp.dot(ids_of, spread, precision=highest, preferred_element_type=F32)
    passage = lax.broadcasted_iota(jnp.int32, (PASSAGES_HERE, 512), 0)
    token = lax.broadcasted_iota(jnp.int32, (PASSAGES_HERE, 512), 1)
    one_hot = ((ids_of == (passage % 4).astype(F32)) & (token // TOK == passage // 4)).astype(F32)
    words = lengths[...].astype(F32)
    average = jnp.sum(words) / 256.0
    words = lax.dot_general(pick, words, NT, precision=highest, preferred_element_type=F32)
    passage = lax.broadcasted_iota(jnp.int32, (PASSAGES_HERE, 4), 0)
    which = lax.broadcasted_iota(jnp.int32, (PASSAGES_HERE, 4), 1)
    words = jnp.sum(jnp.where(which == passage % 4, words, 0.0), axis=1, keepdims=True)
    scale = 1.0 - 0.75 + 0.75 * words / average

    weights[3].wait()
    arrived(to_planes)
    h1, h2, h3 = {}, {}, []

    def pair(i):
        return pl.ds(((x + 1 + i) % 4) * 2, 2)

    def spread_first(i):
        block = LG.at[pair(i), y, c]
        h1[i] = [send(block, block, at(dy=n)) for n in (2, 1, 3)]

    def spread_cores(i):
        arrived(h1[i])
        block = LG.at[pair(i), :, c]
        h2[i] = [send(block, block, at(dc=1))]

    def logits(i):
        arrived(h2[i])
        here = LG[pair(i)].reshape(512, WIDTH)
        return lax.dot_general(here, HW[...], NT, preferred_element_type=F32)

    def head_part(i):
        LS[i] = logits(i).astype(BF16)
        h3.append(send(LS.at[i], LR.at[i], at(dx=1 + i)))

    spread_first(0)
    spread_first(1)
    spread_cores(0)
    spread_first(2)
    head_part(0)
    spread_cores(1)
    spread_first(3)
    head_part(1)
    spread_cores(2)
    head_part(2)
    spread_cores(3)
    total = logits(3)
    arrived(h3)
    for i in range(3):
        total = total + LR[i].astype(F32)
    saturated = jnp.log1p(jnp.maximum(total, 0.0))
    freq = jnp.dot(one_hot, saturated, precision=highest, preferred_element_type=F32)
    out[...] = freq * (1.2 + 1.0) / (freq + 1.2 * scale)

    for copy in copies:
        copy.wait_send()


def local(
    tokens, expert_routes, gate_scores, w_gate, w_up, w_down, head_weight, passage_ids, doc_length
):
    vmem, anywhere = pl.BlockSpec(memory_space=pltpu.VMEM), pl.BlockSpec(memory_space=pl.ANY)
    hidden_units, terms = w_gate.shape[2], head_weight.shape[1]

    def buffer(*shape):
        return pltpu.VMEM(shape, BF16)

    return pl.pallas_call(
        kernel,
        out_shape=jax.ShapeDtypeStruct((PASSAGES_HERE, terms), F32),
        in_specs=[vmem] * 3 + [anywhere] * 4 + [vmem] * 2,
        out_specs=vmem,
        scratch_shapes=[
            buffer(1024, FEATURES),
            buffer(1024, FEATURES),
            buffer(512, FEATURES),
            buffer(512, FEATURES),
            buffer(CHUNKS, 3, CAP, FEATURES),
            buffer(CHUNKS, 3, 64, WIDTH),
            buffer(CHUNKS, CAP, FEATURES),
            buffer(CHUNKS, 64, WIDTH),
            buffer(CHUNKS, 3, CAP, WIDTH),
            buffer(CHUNKS, 3, CAP, WIDTH),
            buffer(CHUNKS, 2, CAP, WIDTH),
            buffer(EXPERTS * CAP, WIDTH),
            buffer(EXPERTS * CAP, WIDTH),
            buffer(hidden_units, FEATURES),
            buffer(hidden_units, FEATURES),
            buffer(hidden_units, FEATURES),
            buffer(terms, WIDTH),
            buffer(8, 4, 2, TOK, WIDTH),
            buffer(3, 512, terms),
            buffer(3, 512, terms),
            pltpu.SemaphoreType.DMA((SENDS,)),
            pltpu.SemaphoreType.DMA((SENDS,)),
            pltpu.SemaphoreType.DMA((4,)),
        ],
        compiler_params=pltpu.CompilerParams(
            collective_id=0, has_side_effects=True, vmem_limit_bytes=60 * 2**20
        ),
        cost_estimate=pl.CostEstimate(
            flops=14_000_000_000, bytes_accessed=13_000_000, transcendentals=800_000
        ),
    )(
        tokens,
        expert_routes.T,
        gate_scores.T,
        w_gate[0].T,
        w_up[0].T,
        w_down[0],
        head_weight.T,
        passage_ids.T,
        doc_length.T,
    )


def solution(mesh):
    in_specs = (
        P("exp", "voc"),
        P("exp", None),
        P("exp", None),
        P("exp", None, "voc"),
        P("exp", None, "voc"),
        P("exp", "voc", None),
        P("voc", "exp"),
        P(),
        P(),
    )
    return jax.shard_map(
        local, mesh=mesh, in_specs=in_specs, out_specs=P("voc", "exp"), check_vma=False
    )
```

```python
import math

import jax
import jax.numpy as jnp
from jax import lax
from jax.experimental import pallas as pl
from jax.experimental.pallas import tpu as pltpu
from jax.sharding import PartitionSpec as P

MESH = pl.DeviceIdType.MESH
BF16, F32 = jnp.bfloat16, jnp.float32
EXPERTS = 8
CAP = 16
TOK = 32
WIDTH = 1024
FEATURES = 4096
CHUNKS = 4
PASSAGES_HERE = 64
SEND_SEMS = 22
RECV_SEMS = 66
NT = (((1,), (1,)), ((), ()))


def aligned(value, step):
    return pl.multiple_of(value, step)


def kernel(
    tok, routes, gates, w_gate, w_up, w_down, head, ids, lengths, out,
    X, PART, PREC, S, QA, VA, RA, QB, VB, RB, TA, TB, RA2, RB2, U, RET, SLOT, WG, WU, WD, HW,
    LG, LS, QX, RX, FS, FR, send_sem, recv_sem, local_sem,
):
    index = lax.axis_index("exp")
    x = lax.axis_index("voc")
    z, y, c = index // 8, (index // 2) % 4, index % 2
    odd = z % 2

    def at(dx=0, dy=0, dz=0, dc=0):
        return (((z + dz + 8) % 8) * 8 + ((y + dy) % 4) * 2 + (c + dc) % 2, (x + dx) % 4)

    weights = [
        pltpu.make_async_copy(src, dst, local_sem.at[i])
        for i, (src, dst) in enumerate([(head, HW.at[odd]), (w_gate, WG), (w_up, WU), (w_down, WD)])
    ]
    for copy in weights:
        copy.start()

    partners = (
        [at(dx=i) for i in (1, 2, 3)]
        + [at(dy=i) for i in (1, 2, 3)]
        + [at(dz=i) for i in range(1, 8)]
        + [at(dc=1)]
    )
    barrier = pltpu.get_barrier_semaphore()
    for partner in partners:
        pl.semaphore_signal(barrier, inc=1, device_id=partner, device_id_type=MESH)

    slot_row = lax.broadcasted_iota(jnp.int32, (EXPERTS * CAP, TOK), 0)
    expert_of, slot_of = slot_row // CAP, slot_row % CAP
    first, second = routes[0:1, :] == expert_of, routes[1:2, :] == expert_of
    hit = (first | second).astype(F32)
    earlier = (
        lax.broadcasted_iota(jnp.int32, (TOK, TOK), 0)
        < lax.broadcasted_iota(jnp.int32, (TOK, TOK), 1)
    ).astype(F32)
    rank = jnp.dot(hit.astype(BF16), earlier.astype(BF16), preferred_element_type=F32)
    place = jnp.where(rank == slot_of.astype(F32), hit, 0.0)
    SLOT[...] = jnp.dot(place.astype(BF16), tok[...], preferred_element_type=F32).astype(BF16)
    gate_of = place * (jnp.where(first, gates[0:1, :], 0.0) + jnp.where(second, gates[1:2, :], 0.0))

    pl.semaphore_wait(barrier, len(partners))

    kinds, stages, singles = {}, [], []
    used = [0, 0]

    def fresh(which):
        used[which] += 1
        return used[which] - 1

    def sized(units):
        if units <= 8:
            return SLOT.at[pl.ds(0, units * 16), :]
        assert units % 4 == 0
        return X.at[pl.ds(0, units * 4), :]

    def remote(src, dst, send_n, recv_n, target):
        return pltpu.make_async_remote_copy(
            src_ref=src, dst_ref=dst, send_sem=send_sem.at[send_n], recv_sem=recv_sem.at[recv_n],
            device_id=target, device_id_type=MESH,
        )

    def stage(kind, moves):
        if kind not in kinds:
            kinds[kind] = [fresh(0), 0]
        recv_n, units = fresh(1), 0
        for src, dst, target in moves:
            remote(src, dst, kinds[kind][0], recv_n, target).start()
            units += math.prod(src.shape) // (16 * WIDTH)
        kinds[kind][1] += units
        return (kinds[kind][0], recv_n, units)

    def arrived(done):
        send_n, recv_n, units = done
        remote(sized(units), sized(units), send_n, recv_n, at(dc=1)).wait_recv()

    def send(src, dst, target):
        copy = remote(src, dst, fresh(0), fresh(1), target)
        copy.start()
        singles.append(copy)
        return copy

    def span(start, step, size=None):
        return pl.ds(aligned(start, step), size or step)

    my_cols = span(x * WIDTH, WIDTH)

    def cols(i):
        return span(((x + i) % 4) * WIDTH, WIDTH)

    def half_cols(i, half):
        return span(((x + i) % 4) * WIDTH + half * 512, 512)

    def rows(k, u, core, yy, count):
        return pl.ds(aligned(((k * 2 + u) * 2 + core) * 64 + (yy % 4) * CAP, CAP), count)

    halves = (pl.ds(0, 2048), pl.ds(2048, 2048))

    def block(k, u):
        return X.at[rows(k, u, c, y, CAP), my_cols]

    from_z = {}
    for k in range(CHUNKS):
        for u, d in ((0, k), (1, 7 - k)):
            if d == 0:
                X[rows(k, u, c, y, CAP), my_cols] = SLOT[span(z * CAP, CAP), :]
            else:
                src = SLOT.at[span(((z + d) % 8) * CAP, CAP), :]
                from_z[k, u] = stage("z", [(src, block(k, u), at(dz=d))])

    a1, a2, ar, a3, d1, r1, rd, rr, r2, r3 = {}, {}, {}, {}, {}, {}, {}, {}, {}, {}

    def gather_first(k):
        if k:
            arrived(from_z[k, 0])
        arrived(from_z[k, 1])
        here, there = block(k, 0), block(k, 1)
        moves = [(here, here, at(dx=i)) for i in (2, 1, 3)]
        a1[k] = stage("a1", moves + [(there, there, at(dy=i)) for i in (2, 1, 3)])

    def gather_second(k):
        arrived(a1[k])
        here, there = X.at[rows(k, 0, c, y, CAP), :], X.at[rows(k, 1, c, 0, 64), my_cols]
        moves = [(here, here, at(dy=i)) for i in (1, 3)]
        a2[k] = stage("a2", moves + [(there, there, at(dx=i)) for i in (1, 3)])

    def gather_relay(k):
        arrived(a2[k])
        moves = []
        for half, (came, goes) in enumerate(((3, 1), (1, 3))):
            block = X.at[rows(k, 0, c, y + came, CAP), halves[half]]
            moves.append((block, block, at(dy=goes)))
            block = X.at[rows(k, 1, c, 0, 64), half_cols(came, half)]
            moves.append((block, block, at(dx=goes)))
        ar[k] = stage("ar", moves)

    def gather_cores(k):
        arrived(ar[k])
        blocks = [X.at[rows(k, u, c, 0, 64), :] for u in (0, 1)]
        a3[k] = stage("a3", [(block, block, at(dc=1)) for block in blocks])

    hidden = {}

    def gate_up(k):
        arrived(a3[k])
        here = X[k * 256 : (k + 1) * 256, :]
        gate_pre = lax.dot_general(here, WG[...], NT, preferred_element_type=F32)
        up_pre = lax.dot_general(here, WU[...], NT, preferred_element_type=F32)
        hidden[k] = (gate_pre / (1.0 + jnp.exp(-gate_pre)) * up_pre).astype(BF16)

    def down(k):
        for n in range(4):
            part = slice(n * WIDTH, (n + 1) * WIDTH)
            PART[k * 256 : (k + 1) * 256, part] = jnp.dot(
                hidden[k], WD[:, part], preferred_element_type=F32
            ).astype(BF16)
        d1[k] = stage("d1", [
            (PART.at[rows(k, u, 1 - c, 0, 64), :], PREC.at[pl.ds((k * 2 + u) * 64, 64), :], at(dc=1))
            for u in (0, 1)
        ])

    def s_rows(k, i):
        return span(k * 128 + ((y + i) % 4) * CAP, CAP)

    def reduce_first(k):
        arrived(d1[k])
        for u in (0, 1):
            to = pl.ds((k * 2 + u) * 64, 64)
            S[to, :] = (
                PART[rows(k, u, c, 0, 64), :].astype(F32) + PREC[to, :].astype(F32)
            ).astype(BF16)
        s64 = pl.ds(k * 128 + 64, 64)
        moves, direct = [], []
        for half, goes in enumerate((1, 3)):
            moves.append((S.at[s_rows(k, 2), halves[half]], QA.at[k, half], at(dy=goes)))
            moves.append((S.at[s64, half_cols(2, half)], QB.at[k, half], at(dx=goes)))
            more = 1 - half
            dst = RA.at[k, half, :, halves[more]]
            direct.append((S.at[s_rows(k, goes), halves[more]], dst, at(dy=goes)))
            dst = RB.at[k, half, :, pl.ds(more * 512, 512)]
            direct.append((S.at[s64, half_cols(goes, more)], dst, at(dx=goes)))
        r1[k] = stage("r1", moves)
        rd[k] = stage("rd", direct)

    def reduce_relay(k):
        arrived(r1[k])
        s64 = pl.ds(k * 128 + 64, 64)
        moves = []
        for half, goes in enumerate((1, 3)):
            VA[k, half] = (
                S[s_rows(k, goes), halves[half]].astype(F32) + QA[k, half].astype(F32)
            ).astype(BF16)
            moves.append((VA.at[k, half], RA.at[k, half, :, halves[half]], at(dy=goes)))
            VB[k, half] = (
                S[s64, half_cols(goes, half)].astype(F32) + QB[k, half].astype(F32)
            ).astype(BF16)
            moves.append((VB.at[k, half], RB.at[k, half, :, pl.ds(half * 512, 512)], at(dx=goes)))
        rr[k] = stage("rr", moves)

    def reduce_second(k):
        arrived(rd[k])
        arrived(rr[k])
        total = S[s_rows(k, 0), :].astype(F32)
        TA[k] = (total + RA[k, 0].astype(F32) + RA[k, 1].astype(F32)).astype(BF16)
        total = S[k * 128 + 64 : k * 128 + 128, my_cols].astype(F32)
        TB[k] = (total + RB[k, 0].astype(F32) + RB[k, 1].astype(F32)).astype(BF16)
        moves = []
        for i in (2, 1, 3):
            moves.append((TA.at[k, :, cols(i)], RA2.at[k, i - 1], at(dx=i)))
            src = TB.at[k, span(((y + i) % 4) * CAP, CAP), :]
            moves.append((src, RB2.at[k, i - 1], at(dy=i)))
        r2[k] = stage("r2", moves)

    mine = span(z * CAP, CAP)

    def give_back(k):
        arrived(r2[k])
        moves = []
        for u, (own, more) in enumerate(
            [(TA[k, :, my_cols], RA2), (TB[k, span(y * CAP, CAP), :], RB2)]
        ):
            total = own.astype(F32)
            for i in range(3):
                total = total + more[k, i].astype(F32)
            if u == 0 and k == 0:
                RET[mine, :] = total.astype(BF16)
            else:
                U[k, u] = total.astype(BF16)
                moves.append((U.at[k, u], RET.at[mine, :], at(dz=-k if u == 0 else 1 + k)))
        r3[k] = stage("r3", moves)

    gather_first(0)
    gather_first(1)
    gather_second(0)
    gather_first(2)
    gather_second(1)
    gather_first(3)
    gather_relay(0)
    gather_second(2)
    weights[0].wait()
    swap = at(dz=1 - 2 * odd)
    head_copy = send(HW.at[odd], HW.at[odd], swap)
    gather_cores(0)
    gather_relay(1)
    gather_second(3)
    for copy in weights[1:]:
        copy.wait()
    gate_up(0)
    gather_cores(1)
    gather_relay(2)
    down(0)
    gate_up(1)
    gather_cores(2)
    gather_relay(3)
    reduce_first(0)
    down(1)
    gate_up(2)
    gather_cores(3)
    reduce_first(1)
    reduce_relay(0)
    down(2)
    gate_up(3)
    reduce_first(2)
    reduce_second(0)
    reduce_relay(1)
    down(3)
    reduce_second(1)
    reduce_relay(2)
    give_back(0)
    reduce_first(3)
    give_back(1)
    reduce_second(2)
    reduce_relay(3)
    give_back(2)
    reduce_second(3)
    give_back(3)

    eye = (
        lax.broadcasted_iota(jnp.int32, (TOK, TOK), 0)
        == lax.broadcasted_iota(jnp.int32, (TOK, TOK), 1)
    ).astype(F32)
    highest = lax.Precision.HIGHEST
    gate_table = lax.dot_general(eye, gate_of, NT, precision=highest, preferred_element_type=F32)
    for k in range(CHUNKS):
        arrived(r3[k])
    moe = jnp.dot(gate_table, RET[...].astype(F32), precision=highest, preferred_element_type=F32)
    LG[z // 2, y, c] = (tok[...].astype(F32) + moe).astype(BF16)

    ours = LG.at[z // 2, y, c]
    to_planes = stage("l0", [(ours, ours, at(dz=d)) for d in (4, 2, 6)])

    def picks(count, first_shard):
        passage = lax.broadcasted_iota(jnp.int32, (count, 64), 0)
        shard = lax.broadcasted_iota(jnp.int32, (count, 64), 1)
        return (shard == passage // 4 + first_shard).astype(F32)

    ids_of = lax.dot_general(
        picks(32, 16 * x + 8 * odd), ids[...].astype(F32), NT,
        precision=highest, preferred_element_type=F32,
    )
    spread = (
        lax.broadcasted_iota(jnp.int32, (TOK, 256), 1) % TOK
        == lax.broadcasted_iota(jnp.int32, (TOK, 256), 0)
    ).astype(F32)
    ids_of = jnp.dot(ids_of, spread, precision=highest, preferred_element_type=F32)
    passage = lax.broadcasted_iota(jnp.int32, (32, 256), 0)
    token = lax.broadcasted_iota(jnp.int32, (32, 256), 1)
    one_hot = ((ids_of == (passage % 4).astype(F32)) & (token // TOK == passage // 4)).astype(F32)
    words = lengths[...].astype(F32)
    average = jnp.sum(words) / 256.0
    words = lax.dot_general(
        picks(PASSAGES_HERE, 16 * x), words, NT, precision=highest, preferred_element_type=F32
    )
    passage = lax.broadcasted_iota(jnp.int32, (PASSAGES_HERE, 4), 0)
    which = lax.broadcasted_iota(jnp.int32, (PASSAGES_HERE, 4), 1)
    words = jnp.sum(jnp.where(which == passage % 4, words, 0.0), axis=1, keepdims=True)
    scale = 1.0 - 0.75 + 0.75 * words / average

    head_copy.wait_recv()
    arrived(to_planes)
    h1, h2 = {}, {}

    def spread_first(i):
        block = LG.at[(x + i) % 4, y, c]
        h1[i] = stage("h1", [(block, block, at(dy=n)) for n in (2, 1, 3)])

    def spread_cores(i):
        arrived(h1[i])
        block = LG.at[(x + i) % 4, :, c]
        h2[i] = stage("h2", [(block, block, at(dc=1))])

    def logits(i):
        arrived(h2[i])
        here = LG[(x + i) % 4].reshape(256, WIDTH)
        return [lax.dot_general(here, HW[v], NT, preferred_element_type=F32) for v in (0, 1)]

    spread_first(2)
    spread_first(1)
    spread_cores(2)
    spread_first(3)
    part = logits(2)
    halfway = []
    for v, goes in enumerate((1, 3)):
        LS[0, v] = part[v].astype(BF16)
        halfway.append(send(LS.at[0, v], QX.at[v], at(dx=goes)))
    spread_cores(1)
    spread_first(0)
    part = logits(1)
    last = []
    LS[1, 1] = part[1].astype(BF16)
    last.append(send(LS.at[1, 1], RX.at[0, 1], at(dx=1)))
    LS[1, 0] = part[0].astype(BF16)
    spread_cores(3)
    part = logits(3)
    LS[2, 0] = part[0].astype(BF16)
    last.append(send(LS.at[2, 0], RX.at[1, 0], at(dx=3)))
    LS[2, 1] = part[1].astype(BF16)
    for v, goes in enumerate((1, 3)):
        halfway[v].wait_recv()
        LS[1 + v, v] = (LS[1 + v, v].astype(F32) + QX[v].astype(F32)).astype(BF16)
        last.append(send(LS.at[1 + v, v], RX.at[v, v], at(dx=goes)))
    spread_cores(0)
    total = logits(0)
    for copy in last:
        copy.wait_recv()
    freq = []
    for v in (0, 1):
        whole = total[v] + RX[0, v].astype(F32) + RX[1, v].astype(F32)
        saturated = jnp.log1p(jnp.maximum(whole, 0.0))
        freq.append(jnp.dot(one_hot, saturated, precision=highest, preferred_element_type=F32))
    FS[...] = jnp.where(odd == 0, freq[1], freq[0])
    FR[odd] = jnp.where(odd == 0, freq[0], freq[1])
    swapped = send(FS, FR.at[odd], swap)
    swapped.wait_recv()
    freq = FR[...].reshape(PASSAGES_HERE, FR.shape[2])
    out[...] = freq * (1.2 + 1.0) / (freq + 1.2 * scale)

    for copy in singles:
        copy.wait_send()
    for send_n, units in kinds.values():
        remote(sized(units), sized(units), send_n, 0, at(dc=1)).wait_send()
    assert used[0] <= SEND_SEMS and used[1] <= RECV_SEMS, used


def local(
    tokens, expert_routes, gate_scores, w_gate, w_up, w_down, head_weight, passage_ids, doc_length
):
    vmem, anywhere = pl.BlockSpec(memory_space=pltpu.VMEM), pl.BlockSpec(memory_space=pl.ANY)
    hidden_units, terms = w_gate.shape[2], head_weight.shape[1]

    def buffer(*shape):
        return pltpu.VMEM(shape, BF16)

    return pl.pallas_call(
        kernel,
        out_shape=jax.ShapeDtypeStruct((PASSAGES_HERE, terms), F32),
        in_specs=[vmem] * 3 + [anywhere] * 4 + [vmem] * 2,
        out_specs=vmem,
        scratch_shapes=[
            buffer(1024, FEATURES),
            buffer(1024, FEATURES),
            buffer(512, FEATURES),
            buffer(512, FEATURES),
            buffer(CHUNKS, 2, CAP, 2048),
            buffer(CHUNKS, 2, CAP, 2048),
            buffer(CHUNKS, 2, CAP, FEATURES),
            buffer(CHUNKS, 2, 64, 512),
            buffer(CHUNKS, 2, 64, 512),
            buffer(CHUNKS, 2, 64, WIDTH),
            buffer(CHUNKS, CAP, FEATURES),
            buffer(CHUNKS, 64, WIDTH),
            buffer(CHUNKS, 3, CAP, WIDTH),
            buffer(CHUNKS, 3, CAP, WIDTH),
            buffer(CHUNKS, 2, CAP, WIDTH),
            buffer(EXPERTS * CAP, WIDTH),
            buffer(EXPERTS * CAP, WIDTH),
            buffer(hidden_units, FEATURES),
            buffer(hidden_units, FEATURES),
            buffer(hidden_units, FEATURES),
            buffer(2, terms, WIDTH),
            buffer(4, 4, 2, TOK, WIDTH),
            buffer(3, 2, 256, terms),
            buffer(2, 256, terms),
            buffer(2, 2, 256, terms),
            pltpu.VMEM((32, terms), F32),
            pltpu.VMEM((2, 32, terms), F32),
            pltpu.SemaphoreType.DMA((SEND_SEMS,)),
            pltpu.SemaphoreType.DMA((RECV_SEMS,)),
            pltpu.SemaphoreType.DMA((4,)),
        ],
        compiler_params=pltpu.CompilerParams(
            collective_id=0, has_side_effects=True, vmem_limit_bytes=60 * 2**20
        ),
        cost_estimate=pl.CostEstimate(
            flops=14_000_000_000, bytes_accessed=13_000_000, transcendentals=800_000
        ),
    )(
        tokens,
        expert_routes.T,
        gate_scores.T,
        w_gate[0].T,
        w_up[0].T,
        w_down[0],
        head_weight.T,
        passage_ids.T,
        doc_length.T,
    )


def solution(mesh):
    in_specs = (
        P("exp", "voc"),
        P("exp", None),
        P("exp", None),
        P("exp", None, "voc"),
        P("exp", None, "voc"),
        P("exp", "voc", None),
        P("voc", "exp"),
        P(),
        P(),
    )
    return jax.shard_map(
        local, mesh=mesh, in_specs=in_specs, out_specs=P("voc", "exp"), check_vma=False
    )
```

```python
import math

import jax
import jax.numpy as jnp
from jax import lax
from jax.experimental import pallas as pl
from jax.experimental.pallas import tpu as pltpu
from jax.sharding import PartitionSpec as P

MESH = pl.DeviceIdType.MESH
BF16, F32 = jnp.bfloat16, jnp.float32
EXPERTS = 8
CAP = 16
TOK = 32
WIDTH = 1024
FEATURES = 4096
CHUNKS = 4
PASSAGES_HERE = 64
SEND_SEMS = 24
RECV_SEMS = 84
NT = (((1,), (1,)), ((), ()))


def aligned(value, step):
    return pl.multiple_of(value, step)


def kernel(
    tok, routes, gates, w_gate, w_up, w_down, head, ids, lengths, out,
    X, PART, PREC, S, QA, VA, RA, QB, VB, RB, TA, TB, RA2, RB2, U, RET, SLOT, WG, WU, WD, HW,
    LG, LS, QX, RX, FS, FR, send_sem, recv_sem, local_sem,
):
    index = lax.axis_index("exp")
    x = lax.axis_index("voc")
    z, y, c = index // 8, (index // 2) % 4, index % 2
    odd = z % 2

    def at(dx=0, dy=0, dz=0, dc=0):
        return (((z + dz + 8) % 8) * 8 + ((y + dy) % 4) * 2 + (c + dc) % 2, (x + dx) % 4)

    weights = [
        pltpu.make_async_copy(src, dst, local_sem.at[i])
        for i, (src, dst) in enumerate([(head, HW.at[odd]), (w_gate, WG), (w_up, WU), (w_down, WD)])
    ]
    for copy in weights:
        copy.start()

    partners = (
        [at(dx=i) for i in (1, 2, 3)]
        + [at(dy=i) for i in (1, 2, 3)]
        + [at(dz=i) for i in range(1, 8)]
        + [at(dc=1)]
    )
    barrier = pltpu.get_barrier_semaphore()
    for partner in partners:
        pl.semaphore_signal(barrier, inc=1, device_id=partner, device_id_type=MESH)

    slot_row = lax.broadcasted_iota(jnp.int32, (EXPERTS * CAP, TOK), 0)
    expert_of, slot_of = slot_row // CAP, slot_row % CAP
    first, second = routes[0:1, :] == expert_of, routes[1:2, :] == expert_of
    hit = (first | second).astype(F32)
    earlier = (
        lax.broadcasted_iota(jnp.int32, (TOK, TOK), 0)
        < lax.broadcasted_iota(jnp.int32, (TOK, TOK), 1)
    ).astype(F32)
    rank = jnp.dot(hit.astype(BF16), earlier.astype(BF16), preferred_element_type=F32)
    place = jnp.where(rank == slot_of.astype(F32), hit, 0.0)
    SLOT[...] = jnp.dot(place.astype(BF16), tok[...], preferred_element_type=F32).astype(BF16)
    gate_of = place * (jnp.where(first, gates[0:1, :], 0.0) + jnp.where(second, gates[1:2, :], 0.0))

    pl.semaphore_wait(barrier, len(partners))

    kinds, stages, singles = {}, [], []
    used = [0, 0]

    def fresh(which):
        used[which] += 1
        return used[which] - 1

    def sized(units):
        if units <= 8:
            return SLOT.at[pl.ds(0, units * 16), :]
        assert units % 4 == 0
        return X.at[pl.ds(0, units * 4), :]

    def remote(src, dst, send_n, recv_n, target):
        return pltpu.make_async_remote_copy(
            src_ref=src, dst_ref=dst, send_sem=send_sem.at[send_n], recv_sem=recv_sem.at[recv_n],
            device_id=target, device_id_type=MESH,
        )

    def stage(kind, moves):
        if kind not in kinds:
            kinds[kind] = [fresh(0), 0]
        recv_n, units = fresh(1), 0
        for src, dst, target in moves:
            remote(src, dst, kinds[kind][0], recv_n, target).start()
            units += math.prod(src.shape) // (16 * WIDTH)
        kinds[kind][1] += units
        return (kinds[kind][0], recv_n, units)

    def arrived(done):
        send_n, recv_n, units = done
        remote(sized(units), sized(units), send_n, recv_n, at(dc=1)).wait_recv()

    def send(src, dst, target):
        copy = remote(src, dst, fresh(0), fresh(1), target)
        copy.start()
        singles.append(copy)
        return copy

    def span(start, step, size=None):
        return pl.ds(aligned(start, step), size or step)

    my_cols = span(x * WIDTH, WIDTH)

    def cols(i):
        return span(((x + i) % 4) * WIDTH, WIDTH)

    def half_cols(i, half):
        return span(((x + i) % 4) * WIDTH + half * 512, 512)

    def rows(k, u, core, yy, count):
        return pl.ds(aligned(((k * 2 + u) * 2 + core) * 64 + (yy % 4) * CAP, CAP), count)

    halves = (pl.ds(0, 2048), pl.ds(2048, 2048))

    def block(k, u):
        return X.at[rows(k, u, c, y, CAP), my_cols]

    from_z = {}
    for k in range(CHUNKS):
        for u, d in ((0, k), (1, 7 - k)):
            if d == 0:
                X[rows(k, u, c, y, CAP), my_cols] = SLOT[span(z * CAP, CAP), :]
            else:
                src = SLOT.at[span(((z + d) % 8) * CAP, CAP), :]
                from_z[k, u] = stage("z", [(src, block(k, u), at(dz=d))])

    a1, a2, ar, a3, d1, r1, rd, rr, r2, r3 = {}, {}, {}, {}, {}, {}, {}, {}, {}, {}

    def gather_first(k):
        if k:
            arrived(from_z[k, 0])
        arrived(from_z[k, 1])
        here, there = block(k, 0), block(k, 1)
        moves = [(here, here, at(dx=i)) for i in (2, 1, 3)]
        a1[k] = stage("a1", moves + [(there, there, at(dy=i)) for i in (2, 1, 3)])

    def gather_second(k):
        arrived(a1[k])
        here, there = X.at[rows(k, 0, c, y, CAP), :], X.at[rows(k, 1, c, 0, 64), my_cols]
        moves = [(here, here, at(dy=i)) for i in (1, 3)]
        a2[k] = stage("a2", moves + [(there, there, at(dx=i)) for i in (1, 3)])

    def gather_relay(k):
        arrived(a2[k])
        moves = []
        for half, (came, goes) in enumerate(((3, 1), (1, 3))):
            block = X.at[rows(k, 0, c, y + came, CAP), halves[half]]
            moves.append((block, block, at(dy=goes)))
            block = X.at[rows(k, 1, c, 0, 64), half_cols(came, half)]
            moves.append((block, block, at(dx=goes)))
        ar[k] = stage("ar", moves)
        a3[k] = [to_core("ac", k, (0, 1, 3))]

    def to_core(kind, k, steps):
        blocks = [X.at[rows(k, 0, c, y + i, CAP), :] for i in steps]
        blocks += [X.at[rows(k, 1, c, 0, 64), cols(i)] for i in steps]
        return stage(kind, [(block, block, at(dc=1)) for block in blocks])

    def gather_cores(k):
        arrived(ar[k])
        a3[k].append(to_core("a3", k, (2,)))

    hidden = {}

    def gate_up(k):
        for done in a3[k]:
            arrived(done)
        here = X[k * 256 : (k + 1) * 256, :]
        gate_pre = lax.dot_general(here, WG[...], NT, preferred_element_type=F32)
        up_pre = lax.dot_general(here, WU[...], NT, preferred_element_type=F32)
        hidden[k] = (gate_pre / (1.0 + jnp.exp(-gate_pre)) * up_pre).astype(BF16)

    def down(k):
        d1[k] = []
        for n in range(4):
            part = slice(n * WIDTH, (n + 1) * WIDTH)
            PART[k * 256 : (k + 1) * 256, part] = jnp.dot(
                hidden[k], WD[:, part], preferred_element_type=F32
            ).astype(BF16)
            part = pl.ds(n * WIDTH, WIDTH)
            moves = []
            for u in (0, 1):
                to = PREC.at[pl.ds((k * 2 + u) * 64, 64), part]
                moves.append((PART.at[rows(k, u, 1 - c, 0, 64), part], to, at(dc=1)))
            d1[k].append(stage("d1", moves))

    def s_rows(k, i):
        return span(k * 128 + ((y + i) % 4) * CAP, CAP)

    def reduce_first(k):
        for n in range(4):
            arrived(d1[k][n])
            part = slice(n * WIDTH, (n + 1) * WIDTH)
            for u in (0, 1):
                to = pl.ds((k * 2 + u) * 64, 64)
                S[to, part] = (
                    PART[rows(k, u, c, 0, 64), part].astype(F32) + PREC[to, part].astype(F32)
                ).astype(BF16)
        s64 = pl.ds(k * 128 + 64, 64)
        moves, direct = [], []
        for half, goes in enumerate((1, 3)):
            moves.append((S.at[s_rows(k, 2), halves[half]], QA.at[k, half], at(dy=goes)))
            moves.append((S.at[s64, half_cols(2, half)], QB.at[k, half], at(dx=goes)))
            more = 1 - half
            dst = RA.at[k, half, :, halves[more]]
            direct.append((S.at[s_rows(k, goes), halves[more]], dst, at(dy=goes)))
            dst = RB.at[k, half, :, pl.ds(more * 512, 512)]
            direct.append((S.at[s64, half_cols(goes, more)], dst, at(dx=goes)))
        r1[k] = stage("r1", moves)
        rd[k] = stage("rd", direct)

    def reduce_relay(k):
        arrived(r1[k])
        s64 = pl.ds(k * 128 + 64, 64)
        moves = []
        for half, goes in enumerate((1, 3)):
            VA[k, half] = (
                S[s_rows(k, goes), halves[half]].astype(F32) + QA[k, half].astype(F32)
            ).astype(BF16)
            moves.append((VA.at[k, half], RA.at[k, half, :, halves[half]], at(dy=goes)))
            VB[k, half] = (
                S[s64, half_cols(goes, half)].astype(F32) + QB[k, half].astype(F32)
            ).astype(BF16)
            moves.append((VB.at[k, half], RB.at[k, half, :, pl.ds(half * 512, 512)], at(dx=goes)))
        rr[k] = stage("rr", moves)

    def reduce_second(k):
        arrived(rd[k])
        arrived(rr[k])
        total = S[s_rows(k, 0), :].astype(F32)
        TA[k] = (total + RA[k, 0].astype(F32) + RA[k, 1].astype(F32)).astype(BF16)
        total = S[k * 128 + 64 : k * 128 + 128, my_cols].astype(F32)
        TB[k] = (total + RB[k, 0].astype(F32) + RB[k, 1].astype(F32)).astype(BF16)
        moves = []
        for i in (2, 1, 3):
            moves.append((TA.at[k, :, cols(i)], RA2.at[k, i - 1], at(dx=i)))
            src = TB.at[k, span(((y + i) % 4) * CAP, CAP), :]
            moves.append((src, RB2.at[k, i - 1], at(dy=i)))
        r2[k] = stage("r2", moves)

    mine = span(z * CAP, CAP)

    def give_back(k):
        arrived(r2[k])
        moves = []
        for u, (own, more) in enumerate(
            [(TA[k, :, my_cols], RA2), (TB[k, span(y * CAP, CAP), :], RB2)]
        ):
            total = own.astype(F32)
            for i in range(3):
                total = total + more[k, i].astype(F32)
            if u == 0 and k == 0:
                RET[mine, :] = total.astype(BF16)
            else:
                U[k, u] = total.astype(BF16)
                moves.append((U.at[k, u], RET.at[mine, :], at(dz=-k if u == 0 else 1 + k)))
        r3[k] = stage("r3", moves)

    gather_first(0)
    gather_first(1)
    gather_second(0)
    gather_first(2)
    gather_second(1)
    gather_first(3)
    gather_relay(0)
    gather_second(2)
    weights[0].wait()
    swap = at(dz=1 - 2 * odd)
    head_copy = send(HW.at[odd], HW.at[odd], swap)
    gather_cores(0)
    gather_relay(1)
    gather_second(3)
    for copy in weights[1:]:
        copy.wait()
    gate_up(0)
    gather_cores(1)
    gather_relay(2)
    down(0)
    gate_up(1)
    gather_cores(2)
    gather_relay(3)
    reduce_first(0)
    down(1)
    gate_up(2)
    gather_cores(3)
    down(2)
    reduce_first(1)
    reduce_relay(0)
    gate_up(3)
    down(3)
    reduce_first(2)
    reduce_relay(1)
    reduce_second(0)
    reduce_first(3)
    reduce_relay(2)
    reduce_second(1)
    reduce_relay(3)
    give_back(0)
    reduce_second(2)
    give_back(1)
    reduce_second(3)
    give_back(2)
    give_back(3)

    eye = (
        lax.broadcasted_iota(jnp.int32, (TOK, TOK), 0)
        == lax.broadcasted_iota(jnp.int32, (TOK, TOK), 1)
    ).astype(F32)
    highest = lax.Precision.HIGHEST
    gate_table = lax.dot_general(eye, gate_of, NT, precision=highest, preferred_element_type=F32)
    for k in range(CHUNKS):
        arrived(r3[k])
    moe = jnp.dot(gate_table, RET[...].astype(F32), precision=highest, preferred_element_type=F32)
    LG[z // 2, y, c] = (tok[...].astype(F32) + moe).astype(BF16)

    ours = LG.at[z // 2, y, c]
    turn = (z // 2 - x + 4) % 4
    l0_send, l0_recv = fresh(0), [fresh(1) for _ in range(4)]

    def to_planes():
        for d in (4, 2, 6):
            remote(ours, ours, l0_send, l0_recv[0] + turn, at(dz=d)).start()

    pl.when(turn == 2)(to_planes)

    def picks(count, first_shard):
        passage = lax.broadcasted_iota(jnp.int32, (count, 64), 0)
        shard = lax.broadcasted_iota(jnp.int32, (count, 64), 1)
        return (shard == passage // 4 + first_shard).astype(F32)

    ids_of = lax.dot_general(
        picks(32, 16 * x + 8 * odd), ids[...].astype(F32), NT,
        precision=highest, preferred_element_type=F32,
    )
    spread = (
        lax.broadcasted_iota(jnp.int32, (TOK, 256), 1) % TOK
        == lax.broadcasted_iota(jnp.int32, (TOK, 256), 0)
    ).astype(F32)
    ids_of = jnp.dot(ids_of, spread, precision=highest, preferred_element_type=F32)
    passage = lax.broadcasted_iota(jnp.int32, (32, 256), 0)
    token = lax.broadcasted_iota(jnp.int32, (32, 256), 1)
    one_hot = ((ids_of == (passage % 4).astype(F32)) & (token // TOK == passage // 4)).astype(F32)
    pl.when(turn != 2)(to_planes)
    words = lengths[...].astype(F32)
    average = jnp.sum(words) / 256.0
    words = lax.dot_general(
        picks(PASSAGES_HERE, 16 * x), words, NT, precision=highest, preferred_element_type=F32
    )
    passage = lax.broadcasted_iota(jnp.int32, (PASSAGES_HERE, 4), 0)
    which = lax.broadcasted_iota(jnp.int32, (PASSAGES_HERE, 4), 1)
    words = jnp.sum(jnp.where(which == passage % 4, words, 0.0), axis=1, keepdims=True)
    scale = 1.0 - 0.75 + 0.75 * words / average

    h1, h2 = {}, {}

    def spread_first(i):
        block = LG.at[(x + i) % 4, y, c]

        @pl.when(turn != i)
        def _():
            remote(block, block, l0_send, l0_recv[i], at(dz=2)).wait_recv()

        h1[i] = stage("h1", [(block, block, at(dy=n)) for n in (2, 1, 3)])

    def spread_cores(i):
        arrived(h1[i])
        block = LG.at[(x + i) % 4, :, c]
        h2[i] = stage("h2", [(block, block, at(dc=1))])

    def logits(i):
        arrived(h2[i])
        here = LG[(x + i) % 4].reshape(256, WIDTH)
        return [lax.dot_general(here, HW[v], NT, preferred_element_type=F32) for v in (0, 1)]

    spread_first(2)
    spread_first(1)
    head_copy.wait_recv()
    spread_cores(2)
    part = logits(2)
    halfway = []
    for v, goes in enumerate((1, 3)):
        LS[0, v] = part[v].astype(BF16)
        halfway.append(send(LS.at[0, v], QX.at[v], at(dx=goes)))
    spread_first(3)
    spread_first(0)
    spread_cores(1)
    part = logits(1)
    last = []
    LS[1, 1] = part[1].astype(BF16)
    last.append(send(LS.at[1, 1], RX.at[0, 1], at(dx=1)))
    LS[1, 0] = part[0].astype(BF16)
    spread_cores(3)
    part = logits(3)
    LS[2, 0] = part[0].astype(BF16)
    last.append(send(LS.at[2, 0], RX.at[1, 0], at(dx=3)))
    LS[2, 1] = part[1].astype(BF16)
    for v, goes in enumerate((1, 3)):
        halfway[v].wait_recv()
        LS[1 + v, v] = (LS[1 + v, v].astype(F32) + QX[v].astype(F32)).astype(BF16)
        last.append(send(LS.at[1 + v, v], RX.at[v, v], at(dx=goes)))
    spread_cores(0)
    total = logits(0)
    for copy in last:
        copy.wait_recv()
    whole = [total[v] + RX[0, v].astype(F32) + RX[1, v].astype(F32) for v in (0, 1)]

    def counts(logits_of):
        saturated = jnp.log1p(jnp.maximum(logits_of, 0.0))
        return jnp.dot(one_hot, saturated, precision=highest, preferred_element_type=F32)

    FS[...] = counts(jnp.where(odd == 0, whole[1], whole[0]))
    swapped = send(FS, FR.at[odd], swap)
    FR[odd] = counts(jnp.where(odd == 0, whole[0], whole[1]))
    swapped.wait_recv()
    freq = FR[...].reshape(PASSAGES_HERE, FR.shape[2])
    out[...] = freq * (1.2 + 1.0) / (freq + 1.2 * scale)

    for copy in singles:
        copy.wait_send()
    remote(sized(6), sized(6), l0_send, 0, at(dc=1)).wait_send()
    for send_n, units in kinds.values():
        remote(sized(units), sized(units), send_n, 0, at(dc=1)).wait_send()
    assert used[0] <= SEND_SEMS and used[1] <= RECV_SEMS, used


def local(
    tokens, expert_routes, gate_scores, w_gate, w_up, w_down, head_weight, passage_ids, doc_length
):
    vmem, anywhere = pl.BlockSpec(memory_space=pltpu.VMEM), pl.BlockSpec(memory_space=pl.ANY)
    hidden_units, terms = w_gate.shape[2], head_weight.shape[1]

    def buffer(*shape):
        return pltpu.VMEM(shape, BF16)

    return pl.pallas_call(
        kernel,
        out_shape=jax.ShapeDtypeStruct((PASSAGES_HERE, terms), F32),
        in_specs=[vmem] * 3 + [anywhere] * 4 + [vmem] * 2,
        out_specs=vmem,
        scratch_shapes=[
            buffer(1024, FEATURES),
            buffer(1024, FEATURES),
            buffer(512, FEATURES),
            buffer(512, FEATURES),
            buffer(CHUNKS, 2, CAP, 2048),
            buffer(CHUNKS, 2, CAP, 2048),
            buffer(CHUNKS, 2, CAP, FEATURES),
            buffer(CHUNKS, 2, 64, 512),
            buffer(CHUNKS, 2, 64, 512),
            buffer(CHUNKS, 2, 64, WIDTH),
            buffer(CHUNKS, CAP, FEATURES),
            buffer(CHUNKS, 64, WIDTH),
            buffer(CHUNKS, 3, CAP, WIDTH),
            buffer(CHUNKS, 3, CAP, WIDTH),
            buffer(CHUNKS, 2, CAP, WIDTH),
            buffer(EXPERTS * CAP, WIDTH),
            buffer(EXPERTS * CAP, WIDTH),
            buffer(hidden_units, FEATURES),
            buffer(hidden_units, FEATURES),
            buffer(hidden_units, FEATURES),
            buffer(2, terms, WIDTH),
            buffer(4, 4, 2, TOK, WIDTH),
            buffer(3, 2, 256, terms),
            buffer(2, 256, terms),
            buffer(2, 2, 256, terms),
            pltpu.VMEM((32, terms), F32),
            pltpu.VMEM((2, 32, terms), F32),
            pltpu.SemaphoreType.DMA((SEND_SEMS,)),
            pltpu.SemaphoreType.DMA((RECV_SEMS,)),
            pltpu.SemaphoreType.DMA((4,)),
        ],
        compiler_params=pltpu.CompilerParams(
            collective_id=0, has_side_effects=True, vmem_limit_bytes=60 * 2**20
        ),
        cost_estimate=pl.CostEstimate(
            flops=14_000_000_000, bytes_accessed=13_000_000, transcendentals=800_000
        ),
    )(
        tokens,
        expert_routes.T,
        gate_scores.T,
        w_gate[0].T,
        w_up[0].T,
        w_down[0],
        head_weight.T,
        passage_ids.T,
        doc_length.T,
    )


def solution(mesh):
    in_specs = (
        P("exp", "voc"),
        P("exp", None),
        P("exp", None),
        P("exp", None, "voc"),
        P("exp", None, "voc"),
        P("exp", "voc", None),
        P("voc", "exp"),
        P(),
        P(),
    )
    return jax.shard_map(
        local, mesh=mesh, in_specs=in_specs, out_specs=P("voc", "exp"), check_vma=False
    )
```

```python
import math

import jax
import jax.numpy as jnp
from jax import lax
from jax.experimental import pallas as pl
from jax.experimental.pallas import tpu as pltpu
from jax.sharding import PartitionSpec as P

MESH = pl.DeviceIdType.MESH
BF16, F32 = jnp.bfloat16, jnp.float32
EXPERTS = 8
CAP = 16
TOK = 32
WIDTH = 1024
FEATURES = 4096
CHUNKS = 4
PASSAGES_HERE = 64
SEND_SEMS = 24
RECV_SEMS = 84
NT = (((1,), (1,)), ((), ()))


def aligned(value, step):
    return pl.multiple_of(value, step)


def kernel(
    tok, routes, gates, w_gate, w_up, w_down, head, ids, lengths, out,
    X, PART, PREC, S, QA, VA, RA, QB, VB, RB, TA, TB, RA2, RB2, U, RET, SLOT, WG, WU, WD, HW,
    LG, LS, QX, RX, FS, FR, send_sem, recv_sem, local_sem,
):
    index = lax.axis_index("exp")
    x = lax.axis_index("voc")
    z, y, c = index // 8, (index // 2) % 4, index % 2
    odd = z % 2

    def at(dx=0, dy=0, dz=0, dc=0):
        return (((z + dz + 8) % 8) * 8 + ((y + dy) % 4) * 2 + (c + dc) % 2, (x + dx) % 4)

    weights = [
        pltpu.make_async_copy(src, dst, local_sem.at[i])
        for i, (src, dst) in enumerate([(head, HW.at[odd]), (w_gate, WG), (w_up, WU), (w_down, WD)])
    ]
    for copy in weights:
        copy.start()

    partners = (
        [at(dx=i) for i in (1, 2, 3)]
        + [at(dy=i) for i in (1, 2, 3)]
        + [at(dz=i) for i in range(1, 8)]
        + [at(dc=1)]
    )
    barrier = pltpu.get_barrier_semaphore()
    for partner in partners:
        pl.semaphore_signal(barrier, inc=1, device_id=partner, device_id_type=MESH)

    slot_row = lax.broadcasted_iota(jnp.int32, (EXPERTS * CAP, TOK), 0)
    expert_of, slot_of = slot_row // CAP, slot_row % CAP
    first, second = routes[0:1, :] == expert_of, routes[1:2, :] == expert_of
    hit = (first | second).astype(F32)
    earlier = (
        lax.broadcasted_iota(jnp.int32, (TOK, TOK), 0)
        < lax.broadcasted_iota(jnp.int32, (TOK, TOK), 1)
    ).astype(F32)
    rank = jnp.dot(hit.astype(BF16), earlier.astype(BF16), preferred_element_type=F32)
    place = jnp.where(rank == slot_of.astype(F32), hit, 0.0)
    SLOT[...] = jnp.dot(place.astype(BF16), tok[...], preferred_element_type=F32).astype(BF16)
    gate_of = place * (jnp.where(first, gates[0:1, :], 0.0) + jnp.where(second, gates[1:2, :], 0.0))

    pl.semaphore_wait(barrier, len(partners))

    kinds, stages, singles = {}, [], []
    used = [0, 0]

    def fresh(which):
        used[which] += 1
        return used[which] - 1

    def sized(units):
        if units <= 8:
            return SLOT.at[pl.ds(0, units * 16), :]
        assert units % 4 == 0
        return X.at[pl.ds(0, units * 4), :]

    def remote(src, dst, send_n, recv_n, target):
        return pltpu.make_async_remote_copy(
            src_ref=src, dst_ref=dst, send_sem=send_sem.at[send_n], recv_sem=recv_sem.at[recv_n],
            device_id=target, device_id_type=MESH,
        )

    def stage(kind, moves):
        if kind not in kinds:
            kinds[kind] = [fresh(0), 0]
        recv_n, units = fresh(1), 0
        for src, dst, target in moves:
            remote(src, dst, kinds[kind][0], recv_n, target).start()
            units += math.prod(src.shape) // (16 * WIDTH)
        kinds[kind][1] += units
        return (kinds[kind][0], recv_n, units)

    def arrived(done):
        send_n, recv_n, units = done
        remote(sized(units), sized(units), send_n, recv_n, at(dc=1)).wait_recv()

    def send(src, dst, target):
        copy = remote(src, dst, fresh(0), fresh(1), target)
        copy.start()
        singles.append(copy)
        return copy

    def span(start, step, size=None):
        return pl.ds(aligned(start, step), size or step)

    my_cols = span(x * WIDTH, WIDTH)

    def cols(i):
        return span(((x + i) % 4) * WIDTH, WIDTH)

    def half_cols(i, half):
        return span(((x + i) % 4) * WIDTH + half * 512, 512)

    def rows(k, u, core, yy, count):
        return pl.ds(aligned(((k * 2 + u) * 2 + core) * 64 + (yy % 4) * CAP, CAP), count)

    halves = (pl.ds(0, 2048), pl.ds(2048, 2048))

    def block(k, u):
        return X.at[rows(k, u, c, y, CAP), my_cols]

    from_z = {}
    for k in range(CHUNKS):
        for u, d in ((0, k), (1, 7 - k)):
            if d == 0:
                X[rows(k, u, c, y, CAP), my_cols] = SLOT[span(z * CAP, CAP), :]
            else:
                src = SLOT.at[span(((z + d) % 8) * CAP, CAP), :]
                from_z[k, u] = stage("z", [(src, block(k, u), at(dz=d))])

    a1, a2, ar, a3, d1, r1, rd, rr, r2, r3 = {}, {}, {}, {}, {}, {}, {}, {}, {}, {}

    def gather_first(k):
        if k:
            arrived(from_z[k, 0])
        arrived(from_z[k, 1])
        here, there = block(k, 0), block(k, 1)
        moves = [(here, here, at(dx=i)) for i in (2, 1, 3)]
        a1[k] = stage("a1", moves + [(there, there, at(dy=i)) for i in (2, 1, 3)])

    def gather_second(k):
        arrived(a1[k])
        here, there = X.at[rows(k, 0, c, y, CAP), :], X.at[rows(k, 1, c, 0, 64), my_cols]
        moves = [(here, here, at(dy=i)) for i in (1, 3)]
        a2[k] = stage("a2", moves + [(there, there, at(dx=i)) for i in (1, 3)])

    def gather_relay(k):
        arrived(a2[k])
        moves = []
        for half, (came, goes) in enumerate(((3, 1), (1, 3))):
            block = X.at[rows(k, 0, c, y + came, CAP), halves[half]]
            moves.append((block, block, at(dy=goes)))
            block = X.at[rows(k, 1, c, 0, 64), half_cols(came, half)]
            moves.append((block, block, at(dx=goes)))
        ar[k] = stage("ar", moves)
        a3[k] = [to_core("ac", k, (0, 1, 3))]

    def to_core(kind, k, steps):
        blocks = [X.at[rows(k, 0, c, y + i, CAP), :] for i in steps]
        blocks += [X.at[rows(k, 1, c, 0, 64), cols(i)] for i in steps]
        return stage(kind, [(block, block, at(dc=1)) for block in blocks])

    def gather_cores(k):
        arrived(ar[k])
        a3[k].append(to_core("a3", k, (2,)))

    hidden = {}

    def gate_up(k):
        for done in a3[k]:
            arrived(done)
        here = X[k * 256 : (k + 1) * 256, :]
        gate_pre = lax.dot_general(here, WG[...], NT, preferred_element_type=F32)
        up_pre = lax.dot_general(here, WU[...], NT, preferred_element_type=F32)
        hidden[k] = (gate_pre / (1.0 + jnp.exp(-gate_pre)) * up_pre).astype(BF16)

    def down(k):
        d1[k] = []
        for n in range(4):
            part = slice(n * WIDTH, (n + 1) * WIDTH)
            PART[k * 256 : (k + 1) * 256, part] = jnp.dot(
                hidden[k], WD[:, part], preferred_element_type=F32
            ).astype(BF16)
            part = pl.ds(n * WIDTH, WIDTH)
            moves = []
            for u in (0, 1):
                to = PREC.at[pl.ds((k * 2 + u) * 64, 64), part]
                moves.append((PART.at[rows(k, u, 1 - c, 0, 64), part], to, at(dc=1)))
            d1[k].append(stage("d1", moves))

    def s_rows(k, i):
        return span(k * 128 + ((y + i) % 4) * CAP, CAP)

    def reduce_first(k):
        for n in range(4):
            arrived(d1[k][n])
            part = slice(n * WIDTH, (n + 1) * WIDTH)
            for u in (0, 1):
                to = pl.ds((k * 2 + u) * 64, 64)
                S[to, part] = (
                    PART[rows(k, u, c, 0, 64), part].astype(F32) + PREC[to, part].astype(F32)
                ).astype(BF16)
        s64 = pl.ds(k * 128 + 64, 64)
        moves, direct = [], []
        for half, goes in enumerate((1, 3)):
            moves.append((S.at[s_rows(k, 2), halves[half]], QA.at[k, half], at(dy=goes)))
            moves.append((S.at[s64, half_cols(2, half)], QB.at[k, half], at(dx=goes)))
            more = 1 - half
            dst = RA.at[k, half, :, halves[more]]
            direct.append((S.at[s_rows(k, goes), halves[more]], dst, at(dy=goes)))
            dst = RB.at[k, half, :, pl.ds(more * 512, 512)]
            direct.append((S.at[s64, half_cols(goes, more)], dst, at(dx=goes)))
        r1[k] = stage("r1", moves)
        rd[k] = stage("rd", direct)

    def reduce_relay(k):
        arrived(r1[k])
        s64 = pl.ds(k * 128 + 64, 64)
        moves = []
        for half, goes in enumerate((1, 3)):
            VA[k, half] = (
                S[s_rows(k, goes), halves[half]].astype(F32) + QA[k, half].astype(F32)
            ).astype(BF16)
            moves.append((VA.at[k, half], RA.at[k, half, :, halves[half]], at(dy=goes)))
            VB[k, half] = (
                S[s64, half_cols(goes, half)].astype(F32) + QB[k, half].astype(F32)
            ).astype(BF16)
            moves.append((VB.at[k, half], RB.at[k, half, :, pl.ds(half * 512, 512)], at(dx=goes)))
        rr[k] = stage("rr", moves)

    def reduce_second(k):
        arrived(rd[k])
        arrived(rr[k])
        total = S[s_rows(k, 0), :].astype(F32)
        TA[k] = (total + RA[k, 0].astype(F32) + RA[k, 1].astype(F32)).astype(BF16)
        total = S[k * 128 + 64 : k * 128 + 128, my_cols].astype(F32)
        TB[k] = (total + RB[k, 0].astype(F32) + RB[k, 1].astype(F32)).astype(BF16)
        moves = []
        for i in (2, 1, 3):
            moves.append((TA.at[k, :, cols(i)], RA2.at[k, i - 1], at(dx=i)))
            src = TB.at[k, span(((y + i) % 4) * CAP, CAP), :]
            moves.append((src, RB2.at[k, i - 1], at(dy=i)))
        r2[k] = stage("r2", moves)

    mine = span(z * CAP, CAP)

    def give_back(k):
        arrived(r2[k])
        moves = []
        for u, (own, more) in enumerate(
            [(TA[k, :, my_cols], RA2), (TB[k, span(y * CAP, CAP), :], RB2)]
        ):
            total = own.astype(F32)
            for i in range(3):
                total = total + more[k, i].astype(F32)
            if u == 0 and k == 0:
                RET[mine, :] = total.astype(BF16)
            else:
                U[k, u] = total.astype(BF16)
                moves.append((U.at[k, u], RET.at[mine, :], at(dz=-k if u == 0 else 1 + k)))
        r3[k] = stage("r3", moves)

    gather_first(0)
    gather_first(1)
    gather_second(0)
    gather_first(2)
    gather_second(1)
    gather_first(3)
    gather_relay(0)
    gather_second(2)
    weights[0].wait()
    swap = at(dz=1 - 2 * odd)
    head_copy = send(HW.at[odd], HW.at[odd], swap)
    gather_cores(0)
    gather_relay(1)
    gather_second(3)
    for copy in weights[1:]:
        copy.wait()
    gate_up(0)
    gather_cores(1)
    gather_relay(2)
    down(0)
    gate_up(1)
    gather_cores(2)
    gather_relay(3)
    reduce_first(0)
    down(1)
    gate_up(2)
    gather_cores(3)
    down(2)
    reduce_first(1)
    reduce_relay(0)
    gate_up(3)
    down(3)
    reduce_first(2)
    reduce_first(3)
    reduce_relay(1)
    reduce_second(0)
    reduce_relay(2)
    reduce_relay(3)
    reduce_second(1)
    give_back(0)
    reduce_second(2)
    reduce_second(3)
    give_back(1)
    give_back(2)
    give_back(3)

    eye = (
        lax.broadcasted_iota(jnp.int32, (TOK, TOK), 0)
        == lax.broadcasted_iota(jnp.int32, (TOK, TOK), 1)
    ).astype(F32)
    highest = lax.Precision.HIGHEST
    gate_table = lax.dot_general(eye, gate_of, NT, precision=highest, preferred_element_type=F32)
    for k in range(CHUNKS):
        arrived(r3[k])
    moe = jnp.dot(gate_table, RET[...].astype(F32), precision=highest, preferred_element_type=F32)
    LG[z // 2, y, c] = (tok[...].astype(F32) + moe).astype(BF16)

    ours = LG.at[z // 2, y, c]
    turn = (z // 2 - x + 4) % 4
    l0_send, l0_recv = fresh(0), [fresh(1) for _ in range(4)]

    def to_planes():
        for d in (4, 2, 6):
            remote(ours, ours, l0_send, l0_recv[0] + turn, at(dz=d)).start()

    pl.when(turn == 2)(to_planes)

    def picks(count, first_shard):
        passage = lax.broadcasted_iota(jnp.int32, (count, 64), 0)
        shard = lax.broadcasted_iota(jnp.int32, (count, 64), 1)
        return (shard == passage // 4 + first_shard).astype(F32)

    ids_of = lax.dot_general(
        picks(32, 16 * x + 8 * odd), ids[...].astype(F32), NT,
        precision=highest, preferred_element_type=F32,
    )
    spread = (
        lax.broadcasted_iota(jnp.int32, (TOK, 256), 1) % TOK
        == lax.broadcasted_iota(jnp.int32, (TOK, 256), 0)
    ).astype(F32)
    ids_of = jnp.dot(ids_of, spread, precision=highest, preferred_element_type=F32)
    passage = lax.broadcasted_iota(jnp.int32, (32, 256), 0)
    token = lax.broadcasted_iota(jnp.int32, (32, 256), 1)
    one_hot = ((ids_of == (passage % 4).astype(F32)) & (token // TOK == passage // 4)).astype(F32)
    pl.when(turn != 2)(to_planes)
    words = lengths[...].astype(F32)
    average = jnp.sum(words) / 256.0
    words = lax.dot_general(
        picks(PASSAGES_HERE, 16 * x), words, NT, precision=highest, preferred_element_type=F32
    )
    passage = lax.broadcasted_iota(jnp.int32, (PASSAGES_HERE, 4), 0)
    which = lax.broadcasted_iota(jnp.int32, (PASSAGES_HERE, 4), 1)
    words = jnp.sum(jnp.where(which == passage % 4, words, 0.0), axis=1, keepdims=True)
    scale = 1.0 - 0.75 + 0.75 * words / average

    h1, h2 = {}, {}

    def spread_first(i):
        block = LG.at[(x + i) % 4, y, c]

        @pl.when(turn != i)
        def _():
            remote(block, block, l0_send, l0_recv[i], at(dz=2)).wait_recv()

        h1[i] = stage("h1", [(block, block, at(dy=n)) for n in (2, 1, 3)])

    def spread_cores(i):
        arrived(h1[i])
        block = LG.at[(x + i) % 4, :, c]
        h2[i] = stage("h2", [(block, block, at(dc=1))])

    def logits(i):
        arrived(h2[i])
        here = LG[(x + i) % 4].reshape(256, WIDTH)
        return [lax.dot_general(here, HW[v], NT, preferred_element_type=F32) for v in (0, 1)]

    spread_first(2)
    spread_first(1)
    head_copy.wait_recv()
    spread_cores(2)
    part = logits(2)
    halfway = []
    for v, goes in enumerate((1, 3)):
        LS[0, v] = part[v].astype(BF16)
        halfway.append(send(LS.at[0, v], QX.at[v], at(dx=goes)))
    spread_first(3)
    spread_first(0)
    spread_cores(1)
    part = logits(1)
    last = []
    LS[1, 1] = part[1].astype(BF16)
    last.append(send(LS.at[1, 1], RX.at[0, 1], at(dx=1)))
    LS[1, 0] = part[0].astype(BF16)
    spread_cores(3)
    part = logits(3)
    LS[2, 0] = part[0].astype(BF16)
    last.append(send(LS.at[2, 0], RX.at[1, 0], at(dx=3)))
    LS[2, 1] = part[1].astype(BF16)
    for v, goes in enumerate((1, 3)):
        halfway[v].wait_recv()
        LS[1 + v, v] = (LS[1 + v, v].astype(F32) + QX[v].astype(F32)).astype(BF16)
        last.append(send(LS.at[1 + v, v], RX.at[v, v], at(dx=goes)))
    spread_cores(0)
    total = logits(0)
    for copy in last:
        copy.wait_recv()
    whole = [total[v] + RX[0, v].astype(F32) + RX[1, v].astype(F32) for v in (0, 1)]

    def counts(logits_of):
        saturated = jnp.log1p(jnp.maximum(logits_of, 0.0))
        return jnp.dot(one_hot, saturated, precision=highest, preferred_element_type=F32)

    FS[...] = counts(jnp.where(odd == 0, whole[1], whole[0]))
    swapped = send(FS, FR.at[odd], swap)
    FR[odd] = counts(jnp.where(odd == 0, whole[0], whole[1]))
    swapped.wait_recv()
    freq = FR[...].reshape(PASSAGES_HERE, FR.shape[2])
    out[...] = freq * (1.2 + 1.0) / (freq + 1.2 * scale)

    for copy in singles:
        copy.wait_send()
    remote(sized(6), sized(6), l0_send, 0, at(dc=1)).wait_send()
    for send_n, units in kinds.values():
        remote(sized(units), sized(units), send_n, 0, at(dc=1)).wait_send()
    assert used[0] <= SEND_SEMS and used[1] <= RECV_SEMS, used


def local(
    tokens, expert_routes, gate_scores, w_gate, w_up, w_down, head_weight, passage_ids, doc_length
):
    vmem, anywhere = pl.BlockSpec(memory_space=pltpu.VMEM), pl.BlockSpec(memory_space=pl.ANY)
    hidden_units, terms = w_gate.shape[2], head_weight.shape[1]

    def buffer(*shape):
        return pltpu.VMEM(shape, BF16)

    return pl.pallas_call(
        kernel,
        out_shape=jax.ShapeDtypeStruct((PASSAGES_HERE, terms), F32),
        in_specs=[vmem] * 3 + [anywhere] * 4 + [vmem] * 2,
        out_specs=vmem,
        scratch_shapes=[
            buffer(1024, FEATURES),
            buffer(1024, FEATURES),
            buffer(512, FEATURES),
            buffer(512, FEATURES),
            buffer(CHUNKS, 2, CAP, 2048),
            buffer(CHUNKS, 2, CAP, 2048),
            buffer(CHUNKS, 2, CAP, FEATURES),
            buffer(CHUNKS, 2, 64, 512),
            buffer(CHUNKS, 2, 64, 512),
            buffer(CHUNKS, 2, 64, WIDTH),
            buffer(CHUNKS, CAP, FEATURES),
            buffer(CHUNKS, 64, WIDTH),
            buffer(CHUNKS, 3, CAP, WIDTH),
            buffer(CHUNKS, 3, CAP, WIDTH),
            buffer(CHUNKS, 2, CAP, WIDTH),
            buffer(EXPERTS * CAP, WIDTH),
            buffer(EXPERTS * CAP, WIDTH),
            buffer(hidden_units, FEATURES),
            buffer(hidden_units, FEATURES),
            buffer(hidden_units, FEATURES),
            buffer(2, terms, WIDTH),
            buffer(4, 4, 2, TOK, WIDTH),
            buffer(3, 2, 256, terms),
            buffer(2, 256, terms),
            buffer(2, 2, 256, terms),
            pltpu.VMEM((32, terms), F32),
            pltpu.VMEM((2, 32, terms), F32),
            pltpu.SemaphoreType.DMA((SEND_SEMS,)),
            pltpu.SemaphoreType.DMA((RECV_SEMS,)),
            pltpu.SemaphoreType.DMA((4,)),
        ],
        compiler_params=pltpu.CompilerParams(
            collective_id=0, has_side_effects=True, vmem_limit_bytes=60 * 2**20
        ),
        cost_estimate=pl.CostEstimate(
            flops=14_000_000_000, bytes_accessed=13_000_000, transcendentals=800_000
        ),
    )(
        tokens,
        expert_routes.T,
        gate_scores.T,
        w_gate[0].T,
        w_up[0].T,
        w_down[0],
        head_weight.T,
        passage_ids.T,
        doc_length.T,
    )


def solution(mesh):
    in_specs = (
        P("exp", "voc"),
        P("exp", None),
        P("exp", None),
        P("exp", None, "voc"),
        P("exp", None, "voc"),
        P("exp", "voc", None),
        P("voc", "exp"),
        P(),
        P(),
    )
    return jax.shard_map(
        local, mesh=mesh, in_specs=in_specs, out_specs=P("voc", "exp"), check_vma=False
    )
```
